256 devices in a mesh: segment: 8 (over z_hi, core), dp: 32 (over y, z_lo, x).
Axes of the slice: x: 4, y: 4, z: 8 (z_hi: 4, z_lo: 2; z = z_hi * 2 + z_lo), core: 2. Of those that a mesh axis runs over, the one named last changes fastest.
Arguments:
- segment_input: bfloat16 [8, 4096, 1536], P('segment', 'dp'), may hold values from -6 to 6
- upstream_grad: bfloat16 [8, 4096, 1536], P('segment', 'dp'), may hold values from -6 to 6
- step_noise: bfloat16 [4096, 1536], P('dp'), may hold values from -6 to 6
- rewards: float32 [4096], P('dp'), may hold values from -4 to 4
- routes: int32 [8, 4096, 2], P('segment', 'dp'), may hold values from 0 to 7, all different within a row
- up_weight: bfloat16 [8, 1536, 24576], P('segment', None, 'dp'), may hold values from -0.15625 to 0.15625
- down_weight: bfloat16 [8, 24576, 1536], P('segment', 'dp'), may hold values from -0.109375 to 0.109375
- router_weight: bfloat16 [8, 1536, 8], P('segment'), may hold values from -0.15625 to 0.15625
- norm_gain: float32 [8, 1536], P('segment'), may hold values from 0.5 to 1.5
Outputs:
- input_grad: bfloat16 [8, 4096, 1536], P('segment', 'dp')
- up_grad: bfloat16 [8, 1536, 24576], P('segment', None, 'dp')
- down_grad: bfloat16 [8, 24576, 1536], P('segment', 'dp')
- router_grad: float32 [8, 1536, 8], P('segment')
- gain_grad: float32 [8, 1536], P('segment')
The draws below stay inside these ranges and needn't reach their ends.
Inputs may be any that keep to these rules, and one draw needn't show every extreme that they name: `routes`: each token names 2 different experts in each layer.
All inputs are finite; a program needn't handle non-finite values.
Results may differ from the reference program's by a relative error of at most 0.0075.
Values may be sent and summed in bfloat16 or wider, within the bound.
No kernel may reach another device: no remote copies, remote signals or barrier semaphores. Data moves between devices by JAX's collectives and lax.ppermute only.
A program may use at most 128 MiB of HBM per device.

```python
import jax
import jax.numpy as jnp
from jax import lax

D = 1536
E = 8
FFW = 3072
TOP = 2
TOK_DEV = 128
CAP = 32
SPLIT = 4
HID_DEV = 768
TOKENS = 4096
LAYERS = 8
N_SEGMENT = 8
N_DP = 32


def level_of(stream_key, extent, cuts, smallest, largest):
    factor_of = 1.0
    for dim, parts in cuts:
        draws = jax.random.uniform(jax.random.fold_in(jax.random.fold_in(stream_key, 6), dim), (parts,), jnp.float32, smallest / len(cuts), largest / len(cuts))
        factor_of = factor_of * jnp.repeat(jnp.exp(draws), extent[dim] // parts).reshape((-1,) + (1,) * (len(extent) - 1 - dim))
    return factor_of


def distinct(key, rows, amount, top, lift):
    ranking = jax.random.permutation(jax.random.fold_in(key, 1), amount)
    pull = ranking
    for power in range(3):
        pull = pull * pull // amount
    pull = pull * lift // amount
    lots = jax.random.randint(jax.random.fold_in(key, 2), (rows, amount), 0, 4096) + pull
    fixed_rows = jax.random.permutation(jax.random.fold_in(key, 3), rows)[jnp.arange(amount) % rows]
    lots = jnp.where(jnp.arange(rows)[:, None] == fixed_rows[None, :], 1 << 14, lots)
    score = lots * amount + jnp.arange(amount)
    return lax.top_k(score.astype(jnp.int32), top)[1].astype(jnp.int32)


def gaussian(key, shape, scale, most, cuts=(), kind=jnp.bfloat16):
    level = level_of(key, shape, cuts, -0.22, 0.18) if cuts else 1.0
    entries = jax.random.normal(key, shape, jnp.float32) * scale * level
    return jnp.minimum(jnp.maximum(entries, -most), most).astype(kind)


def setup_inputs(seed: int = 0) -> dict:
    keys = jax.random.split(jax.random.key(seed), 10)
    segment_input = gaussian(keys[0], (LAYERS, TOKENS, D), 1.0, 6.0, ((0, 8), (1, 32)))
    upstream_grad = gaussian(keys[1], (LAYERS, TOKENS, D), 1.0, 6.0, ((0, 8), (1, 32)))
    step_noise = gaussian(keys[2], (TOKENS, D), 1.0, 6.0, ((0, 32),))
    rewards = gaussian(keys[3], (TOKENS,), 1.0, 4.0, ((0, 32),), jnp.float32)
    routes = distinct(keys[4], LAYERS * TOKENS, E, TOP, 4096).reshape((LAYERS, TOKENS, TOP))
    up_weight = gaussian(keys[5], (LAYERS, D, E * FFW), D ** -0.5, 0.15625, ((0, 8), (2, 32)))
    down_weight = gaussian(keys[6], (LAYERS, E * FFW, D), FFW ** -0.5, 0.109375, ((0, 8), (1, 32)))
    router_weight = gaussian(keys[7], (LAYERS, D, E), D ** -0.5, 0.15625, ((0, 8),))
    norm_gain = jnp.clip(1.0 + 0.1 * jax.random.normal(keys[8], (LAYERS, D), jnp.float32), 0.5, 1.5)
    return {"segment_input": segment_input, "upstream_grad": upstream_grad, "step_noise": step_noise, "rewards": rewards, "routes": routes, "up_weight": up_weight, "down_weight": down_weight, "router_weight": router_weight, "norm_gain": norm_gain}


gelu_scale = 0.7978845608028654
cubic_coef = 0.044715
norm_eps = 1e-06

def gelu_tanh(values):
    inner = gelu_scale * (values + cubic_coef * values * values * values)
    return 0.5 * values * (1.0 + jnp.tanh(inner))

def gelu_slope(values):
    inner = gelu_scale * (values + cubic_coef * values * values * values)
    tangent = jnp.tanh(inner)
    return 0.5 * (1.0 + tangent) + 0.5 * values * (1.0 - tangent * tangent) * gelu_scale * (1.0 + 3.0 * cubic_coef * values * values)

def rounded(values):
    return lax.optimization_barrier(values.astype(jnp.bfloat16)).astype(jnp.float32)

def block_slots(block_routes):
    onehot = (block_routes[:, :, None] == jnp.arange(E, dtype=jnp.int32)[None, None, :]).astype(jnp.int32)
    onehot = onehot.reshape(TOK_DEV * TOP, E)
    before = jnp.cumsum(onehot, 0) - onehot
    position = lax.optimization_barrier(jnp.sum(before * onehot, -1))
    expert_id = block_routes.reshape(-1)
    slot_index = jnp.where(position < CAP, expert_id * CAP + position, E * CAP).astype(jnp.int32)
    pair_ids = jnp.arange(TOK_DEV * TOP, dtype=jnp.int32)
    pair_of_slot = jnp.full((E * CAP + 1,), TOK_DEV * TOP, jnp.int32).at[slot_index].set(pair_ids)[:E * CAP]
    return (slot_index, pair_of_slot)

def pick_rows(table, index):
    return table[index]

def per_expert(pieces):
    rows_e, cot_e, gate_e, up_e, down_e = pieces
    rows32 = rows_e.reshape(-1, D).astype(jnp.float32)
    up32 = up_e.astype(jnp.float32)
    down32 = down_e.astype(jnp.float32)
    pre = jnp.einsum('rd,dqf->qrf', rows32, up32)
    hidden = rounded(gelu_tanh(pre))
    partial_value = rounded(jnp.einsum('qrf,qfd->qrd', hidden, down32))
    outputs = lax.optimization_barrier(jnp.sum(partial_value, 0))
    scaled = rounded(gate_e.reshape(-1, 1).astype(jnp.float32) * cot_e.reshape(-1, D).astype(jnp.float32))
    down_g = jnp.einsum('qrf,rd->qfd', hidden, scaled)
    d_hidden = jnp.einsum('rd,qfd->qrf', scaled, down32)
    d_pre = rounded(d_hidden * gelu_slope(pre))
    up_g = jnp.einsum('rd,qrf->dqf', rows32, d_pre)
    back = rounded(jnp.einsum('qrf,dqf->qrd', d_pre, up32))
    return (outputs, lax.optimization_barrier(jnp.sum(back, 0)), up_g.astype(jnp.bfloat16), down_g.astype(jnp.bfloat16))

def layer_backward(layer_input, cotangent, layer_routes, up_w, down_w, router_w, norm_scale_vector):
    input_float32 = layer_input.astype(jnp.float32)
    reciprocal_root_mean = lax.rsqrt(lax.optimization_barrier(jnp.mean(input_float32 * input_float32, -1, keepdims=True)) + norm_eps)
    unit_norm_rows = input_float32 * reciprocal_root_mean
    rescaled_rows = (unit_norm_rows * norm_scale_vector[None, :]).astype(jnp.bfloat16)
    logits = jnp.dot(rescaled_rows, router_w, preferred_element_type=jnp.float32)
    onehot = (layer_routes[:, :, None] == jnp.arange(E, dtype=jnp.int32)[None, None, :]).astype(jnp.float32)
    chosen = lax.optimization_barrier(jnp.sum(logits[:, None, :] * onehot, -1))
    first_gate = jax.nn.sigmoid(chosen[:, 0] - chosen[:, 1])
    gates = jnp.stack([first_gate, 1.0 - first_gate], 1)
    slot_index, pair_of_slot = jax.vmap(block_slots)(layer_routes.reshape(N_DP, TOK_DEV, TOP))
    token_of_slot = pair_of_slot // TOP
    picker = jax.vmap(pick_rows)
    normed_pad = jnp.concatenate([rescaled_rows.reshape(N_DP, TOK_DEV, D), jnp.zeros((N_DP, 1, D), jnp.bfloat16)], 1)
    cot_pad = jnp.concatenate([cotangent.reshape(N_DP, TOK_DEV, D), jnp.zeros((N_DP, 1, D), jnp.bfloat16)], 1)
    gate_pad = jnp.concatenate([gates.reshape(N_DP, TOK_DEV * TOP), jnp.zeros((N_DP, 1), jnp.float32)], 1)
    sent_rows = picker(normed_pad, token_of_slot).reshape(N_DP, E, CAP, D).transpose(1, 0, 2, 3)
    sent_cot = picker(cot_pad, token_of_slot).reshape(N_DP, E, CAP, D).transpose(1, 0, 2, 3)
    sent_gate = picker(gate_pad, pair_of_slot).astype(jnp.bfloat16).reshape(N_DP, E, CAP).transpose(1, 0, 2)
    up_split = up_w.reshape(D, E, SPLIT, HID_DEV).transpose(1, 0, 2, 3)
    down_split = down_w.reshape(E, SPLIT, HID_DEV, D)
    outputs, backs, up_g, down_g = lax.map(per_expert, (sent_rows, sent_cot, sent_gate, up_split, down_split))
    out_slots = outputs.reshape(E, N_DP, CAP, D).transpose(1, 0, 2, 3).reshape(N_DP, E * CAP, D)
    back_slots = backs.reshape(E, N_DP, CAP, D).transpose(1, 0, 2, 3).reshape(N_DP, E * CAP, D)
    zero_row = jnp.zeros((N_DP, 1, D), jnp.float32)
    out_pair = picker(jnp.concatenate([out_slots, zero_row], 1), slot_index)
    back_pair = picker(jnp.concatenate([back_slots, zero_row], 1), slot_index)
    cot_pair = jnp.broadcast_to(cotangent.astype(jnp.float32).reshape(N_DP, TOK_DEV, 1, D), (N_DP, TOK_DEV, TOP, D))
    d_gate = lax.optimization_barrier(jnp.sum(out_pair * cot_pair.reshape(N_DP, TOK_DEV * TOP, D), -1)).reshape(TOKENS, TOP)
    expert_dx = lax.optimization_barrier(jnp.sum(back_pair.reshape(TOKENS, TOP, D), 1))
    d_logit = first_gate * (1.0 - first_gate) * (d_gate[:, 0] - d_gate[:, 1])
    d_logits = (onehot[:, 0, :] - onehot[:, 1, :]) * d_logit[:, None]
    router_g = jnp.dot(rescaled_rows.astype(jnp.float32).T, d_logits, precision=lax.Precision.HIGHEST)
    normed_cotangent = expert_dx + jnp.dot(d_logits, router_w.astype(jnp.float32).T, precision=lax.Precision.HIGHEST)
    scale_vector_grad = lax.optimization_barrier(jnp.sum(normed_cotangent * unit_norm_rows, 0))
    unit_rows_grad = normed_cotangent * norm_scale_vector[None, :]
    input_cotangent = reciprocal_root_mean * (unit_rows_grad - unit_norm_rows * lax.optimization_barrier(jnp.mean(unit_rows_grad * unit_norm_rows, -1, keepdims=True)))
    input_g = (cotangent.astype(jnp.float32) + input_cotangent).astype(jnp.bfloat16)
    up_full = up_g.transpose(1, 0, 2, 3).reshape(D, E * FFW)
    down_full = down_g.reshape(E * FFW, D)
    return (input_g, up_full, down_full, router_g, scale_vector_grad)

def reference(segment_input, upstream_grad, step_noise, rewards, routes, up_weight, down_weight, router_weight, norm_gain):
    results = []
    for layer in range(N_SEGMENT):
        if layer < N_SEGMENT - 1:
            cotangent = upstream_grad[layer + 1]
        else:
            cotangent = (-rewards[:, None] * step_noise.astype(jnp.float32)).astype(jnp.bfloat16)
        results.append(layer_backward(segment_input[layer], cotangent, routes[layer], up_weight[layer], down_weight[layer], router_weight[layer], norm_gain[layer]))
    input_grad = jnp.stack([item[0] for item in results])
    up_grad = jnp.stack([item[1] for item in results])
    down_grad = jnp.stack([item[2] for item in results])
    router_grad = jnp.stack([item[3] for item in results])
    gain_grad = jnp.stack([item[4] for item in results])
    return (input_grad, up_grad, down_grad, router_grad, gain_grad)
```

```python
import jax
import jax.numpy as jnp
from jax import lax
from jax.sharding import Mesh, PartitionSpec as P

gelu_scale = 0.7978845608028654
cubic_coef = 0.044715
norm_eps = 1e-06
bf16 = jnp.bfloat16
f32 = jnp.float32


def shift(value, axis, steps):
    count = lax.axis_size(axis)
    return lax.ppermute(value, axis, [(i, (i + steps) % count) for i in range(count)])


def swap(value, axis, mask):
    count = lax.axis_size(axis)
    return lax.ppermute(value, axis, [(i, i ^ mask) for i in range(count)])


def total_over(value):
    for axis in ("x", "e"):
        mask = 1
        while mask < lax.axis_size(axis):
            value = value + swap(value, axis, mask)
            mask *= 2
    return value


def dot(a, b, dims):
    return lax.dot_general(a, b, (dims, ((), ())), preferred_element_type=f32)


def gather_x(rows):
    half = rows.shape[0] // 2
    low = shift(rows, "x", 1)
    high = shift(rows, "x", -1)
    far_low = shift(low[:half], "x", 1)
    far_high = shift(high[half:], "x", -1)
    return [rows, low, high, far_low, far_high]


def scatter_x(parts):
    own, low, high, far_low, far_high = parts
    half = own.shape[0] // 2
    got_low = shift(far_low.astype(bf16), "x", -1)
    got_high = shift(far_high.astype(bf16), "x", 1)
    low_b = shift(low[half:].astype(bf16), "x", -1)
    high_a = shift(high[:half].astype(bf16), "x", 1)
    high_b = shift((high[half:] + got_high.astype(f32)).astype(bf16), "x", 1)
    low_a = shift((low[:half] + got_low.astype(f32)).astype(bf16), "x", -1)
    first = own[:half] + high_a.astype(f32) + low_a.astype(f32)
    second = own[half:] + high_b.astype(f32) + low_b.astype(f32)
    return jnp.concatenate([first.astype(bf16), second.astype(bf16)], 0)


def relative(table):
    count = table.shape[1]
    here = lax.axis_index("x")
    steps = jnp.array([0, -1, 1, 2], jnp.int32)
    place = (here + steps) % count
    pick = (place[:, None] == jnp.arange(count)[None, :]).astype(f32)
    return pick


def shards(
    segment_input,
    upstream_grad,
    step_noise,
    rewards,
    routes,
    up_weight,
    down_weight,
    router_weight,
    norm_gain,
):
    tok_count = segment_input.shape[1]
    width = segment_input.shape[2]
    experts = router_weight.shape[2]
    split = lax.axis_size("x")
    top_count = routes.shape[2]
    capacity = tok_count * top_count // experts
    slots = experts * capacity
    up = up_weight[0]
    down = down_weight[0]
    router = router_weight[0]
    gain = norm_gain[0]
    n_segment = lax.axis_size("segment")
    arrived = lax.ppermute(
        upstream_grad[0], "segment", [(i + 1, i) for i in range(n_segment - 1)]
    )
    own_grad = (-rewards[:, None] * step_noise.astype(f32)).astype(bf16)
    is_last = lax.axis_index("segment") == n_segment - 1
    cot = jnp.where(is_last, own_grad, arrived)

    x32 = segment_input[0].astype(f32)
    inv = lax.rsqrt(jnp.mean(x32 * x32, -1, keepdims=True) + norm_eps)
    xh = x32 * inv
    xn = (xh * gain[None, :]).astype(bf16)
    logits = dot(router, xn, ((0,), (1,)))
    ids = jnp.arange(experts, dtype=jnp.int32)[:, None]
    first = (routes[0, :, 0][None, :] == ids).astype(f32)
    second = (routes[0, :, 1][None, :] == ids).astype(f32)
    named = first + second
    g1 = jax.nn.sigmoid(
        jnp.sum(first * logits, 0, keepdims=True) - jnp.sum(second * logits, 0, keepdims=True)
    )
    gates = first * g1 + second * (1.0 - g1)
    earlier = (jnp.arange(tok_count)[:, None] < jnp.arange(tok_count)[None, :]).astype(bf16)
    place = dot(named.astype(bf16), earlier, ((1,), (0,)))
    place = jnp.where(named > 0, place, -1.0)
    chosen = place[:, None, :] == jnp.arange(capacity, dtype=f32)[None, :, None]
    pick = chosen.astype(bf16).reshape(slots, tok_count)
    gate_slot = jnp.sum(jnp.where(chosen, gates[:, None, :], 0.0), -1)

    xn_slots = dot(pick, xn, ((1,), (0,))).astype(bf16).reshape(experts, capacity, width)
    c_slots = dot(pick, cot, ((1,), (0,))).astype(bf16).reshape(experts, capacity, width)
    xn_got = lax.all_to_all(xn_slots, "e", 0, 0, tiled=True).reshape(slots, width)
    xn_parts = gather_x(xn_got)
    c_got = lax.all_to_all(c_slots, "e", 0, 0, tiled=True).reshape(slots, width)
    c_parts = gather_x(c_got)

    spread = jnp.broadcast_to(gate_slot[:, None, :], (experts, split, capacity)).reshape(
        experts * split, capacity
    )
    gate_got = lax.all_to_all(spread, ("e", "x"), 0, 0, tiled=True)
    gate_got = gate_got.reshape(experts, split, capacity)
    turn = relative(gate_got)
    gate_rel = jnp.einsum(
        "rx,exc->rec", turn, gate_got, precision=lax.Precision.HIGHEST
    ).reshape(split * slots)

    hs, ds, backs, dgs = [], [], [], []
    for xn_c, c_c in zip(xn_parts, c_parts):
        pre = dot(xn_c, up, ((1,), (0,)))
        square = pre * pre
        tangent = jnp.tanh(gelu_scale * pre * (1.0 + cubic_coef * square))
        hidden = (0.5 * pre * (1.0 + tangent)).astype(bf16)
        slope = 0.5 * (1.0 + tangent) + 0.5 * pre * (1.0 - tangent * tangent) * gelu_scale * (
            1.0 + 3.0 * cubic_coef * square
        )
        dh = dot(c_c, down, ((1,), (1,)))
        dgs.append(jnp.sum(hidden.astype(f32) * dh, -1))
        d_pre = (dh * slope).astype(bf16)
        backs.append(dot(d_pre, up, ((1,), (1,))))
        hs.append(hidden)
        ds.append(d_pre)
    half = slots // 2
    dg = jnp.concatenate(dgs, 0).reshape(split, experts, capacity)
    dg_abs = jnp.einsum("rx,rec->exc", turn, dg, precision=lax.Precision.HIGHEST)
    dg_got = lax.all_to_all(
        dg_abs.reshape(experts * split, capacity), ("e", "x"), 0, 0, tiled=True
    )
    dg_slot = jnp.sum(dg_got.reshape(experts, split, capacity), 1)

    back = scatter_x(backs).reshape(experts, capacity, width)
    back_slots = lax.all_to_all(back, "e", 0, 0, tiled=True).reshape(slots, width)

    gate_col = gate_rel[:, None]
    h_all = (jnp.concatenate(hs, 0).astype(f32) * gate_col).astype(bf16)
    d_all = (jnp.concatenate(ds, 0).astype(f32) * gate_col).astype(bf16)
    xn_all = jnp.concatenate(xn_parts, 0)
    c_all = jnp.concatenate(c_parts, 0)
    down_g = dot(h_all, c_all, ((0,), (0,)))
    up_g = dot(xn_all, d_all, ((0,), (0,)))
    gain_part = jnp.sum(up_g * up.astype(f32), 1)

    dg_tok = jnp.sum(jnp.where(chosen, dg_slot[:, :, None], 0.0), 1)
    dl = g1 * (1.0 - g1) * jnp.sum((first - second) * dg_tok, 0, keepdims=True)
    d_logits = (first - second) * dl
    router_part = lax.dot_general(
        d_logits,
        xn.astype(f32),
        (((1,), (0,)), ((), ())),
        precision=lax.Precision.HIGHEST,
    )
    small = total_over(jnp.concatenate([router_part, gain_part[None, :]], 0))
    router_total = small[:experts]
    router32 = router.astype(f32)
    gain_total = (small[experts] + jnp.sum(router_total * router32.T, 0)) / gain

    weigh = jnp.where(chosen, gates[:, None, :], 0.0).astype(bf16).reshape(slots, tok_count)
    dxe = dot(weigh, back_slots, ((0,), (0,)))
    dxn = dxe + lax.dot_general(
        d_logits, router32, (((0,), (1,)), ((), ())), precision=lax.Precision.HIGHEST
    )
    dh_row = dxn * gain[None, :]
    input_g = cot.astype(f32) + inv * (
        dh_row - xh * jnp.mean(dh_row * xh, -1, keepdims=True)
    )
    return (
        input_g.astype(bf16)[None],
        up_g.astype(bf16)[None],
        down_g.astype(bf16)[None],
        router_total.T[None],
        gain_total[None],
    )


def solution(mesh):
    experts = 8
    n_segment, n_dp = mesh.devices.shape
    grid = Mesh(
        mesh.devices.reshape(n_segment, experts, n_dp // experts), ("segment", "e", "x")
    )
    dp = ("e", "x")
    return jax.shard_map(
        shards,
        mesh=grid,
        in_specs=(
            P("segment", dp, None),
            P("segment", dp, None),
            P(dp, None),
            P(dp),
            P("segment", dp, None),
            P("segment", None, dp),
            P("segment", dp, None),
            P("segment", None, None),
            P("segment", None),
        ),
        out_specs=(
            P("segment", dp, None),
            P("segment", None, dp),
            P("segment", dp, None),
            P("segment", None, None),
            P("segment", None),
        ),
        check_vma=False,
    )
```

```python
import functools

import jax
import jax.numpy as jnp
from jax import lax
from jax.experimental import pallas as pl
from jax.experimental.pallas import tpu as pltpu
from jax.sharding import Mesh, PartitionSpec as P

gelu_scale = 0.7978845608028654
cubic_coef = 0.044715
norm_eps = 1e-06
lane = 128
bf16 = jnp.bfloat16
f32 = jnp.float32
room = 60 << 20
cheaper = 8


def shift(value, axis, steps):
    count = lax.axis_size(axis)
    return lax.ppermute(value, axis, [(i, (i + steps) % count) for i in range(count)])


def swap(value, axis, mask):
    count = lax.axis_size(axis)
    return lax.ppermute(value, axis, [(i, i ^ mask) for i in range(count)])


def total_over(value):
    value = value + swap(value, "e", 1)
    for axis, unit in (("e", 2), ("x", 1)):
        one, two, three = (swap(value, axis, unit * mask) for mask in (1, 2, 3))
        value = (value + two) + (one + three)
    return value


def after(value, *done):
    return lax.optimization_barrier((value,) + done)[0]


def dot(a, b, dims):
    return lax.dot_general(a, b, (dims, ((), ())), preferred_element_type=f32)


def exact(a, b, dims):
    return lax.dot_general(
        a, b, (dims, ((), ())), preferred_element_type=f32, precision=lax.Precision.HIGHEST
    )


def like(shape, dtype):
    return jax.ShapeDtypeStruct(shape, dtype)


def call(kernel, out, flops, moved, **options):
    return pl.pallas_call(
        kernel,
        out_shape=out,
        cost_estimate=pl.CostEstimate(flops=flops, bytes_accessed=moved, transcendentals=0),
        compiler_params=pltpu.CompilerParams(vmem_limit_bytes=room),
        **options,
    )


def one_hots(routes, experts, tok_count):
    ids = lax.broadcasted_iota(jnp.int32, (experts, tok_count), 0)
    return (ids == routes[0:1, :]).astype(f32), (ids == routes[1:2, :]).astype(f32)


def token_kernel(
    capacity, x_ref, gain_ref, router_ref, routes_ref, xn_ref, slots_ref, pick_ref, gate_ref, back_ref, g_ref
):
    tok_count = x_ref.shape[0]
    experts = router_ref.shape[0]
    slots = experts * capacity
    x32 = x_ref[...].astype(f32)
    inv = lax.rsqrt(jnp.mean(x32 * x32, -1, keepdims=True) + norm_eps)
    xn = (x32 * inv * gain_ref[...]).astype(bf16)
    xn_ref[...] = xn
    logits = dot(router_ref[...], xn, ((1,), (1,)))
    first, second = one_hots(routes_ref[...], experts, tok_count)
    named = first + second
    g1 = jax.nn.sigmoid(
        jnp.sum(first * logits, 0, keepdims=True) - jnp.sum(second * logits, 0, keepdims=True)
    )
    g_ref[...] = g1
    gates = first * g1 + second * (1.0 - g1)
    row = lax.broadcasted_iota(jnp.int32, (tok_count, tok_count), 0)
    col = lax.broadcasted_iota(jnp.int32, (tok_count, tok_count), 1)
    earlier = (row < col).astype(f32).astype(bf16)
    place = dot(named.astype(bf16), earlier, ((1,), (0,)))
    place = jnp.where(named > 0, place, -1.0)
    slot = lax.broadcasted_iota(jnp.int32, (capacity, tok_count), 0).astype(f32)
    chosen = jnp.concatenate(
        [(slot == place[e : e + 1, :]).astype(f32) for e in range(experts)], 0
    )
    spread = jnp.concatenate(
        [jnp.broadcast_to(gates[e : e + 1, :], (capacity, tok_count)) for e in range(experts)], 0
    )
    pick = chosen.astype(bf16)
    pick_ref[...] = pick
    weighed = chosen * spread
    gate = jnp.sum(weighed, -1, keepdims=True)
    gate_ref[...] = jnp.broadcast_to(gate, (slots, lane)).astype(bf16)
    back_ref[...] = weighed.T.astype(bf16)
    slots_ref[...] = dot(pick, xn, ((1,), (0,))).astype(bf16)


def cot_kernel(last_ref, arrived_ref, noise_ref, rewards_ref, pick_ref, gate_ref, cot_ref, slots_ref):
    width = arrived_ref.shape[1]
    own = (-rewards_ref[...] * noise_ref[...].astype(f32)).astype(bf16)
    last = last_ref[0] == 1
    cot = jnp.where(last, own.astype(f32), arrived_ref[...].astype(f32)).astype(bf16)
    cot_ref[...] = cot
    slots_ref[:, :width] = dot(pick_ref[...], cot, ((1,), (0,))).astype(bf16)
    slots_ref[:, width:] = gate_ref[...]


def as_row(column):
    return jnp.broadcast_to(column, (column.shape[0], lane)).T[0:1, :]


def expert_rows(xn, cot, gate, up, down):
    pre = dot(xn, up, ((1,), (0,)))
    dh = dot(cot, down, ((1,), (1,)))
    square = pre * pre
    tangent = jnp.tanh(gelu_scale * pre * (1.0 + cubic_coef * square))
    hidden = 0.5 * pre * (1.0 + tangent)
    slope = 0.5 * (1.0 + tangent) + 0.5 * pre * (1.0 - tangent * tangent) * gelu_scale * (
        1.0 + 3.0 * cubic_coef * square
    )
    hidden = hidden.astype(bf16).astype(f32)
    d_gate = jnp.sum(hidden * dh, -1, keepdims=True)
    d_pre = dh * slope
    back = dot(d_pre.astype(bf16), up, ((1,), (1,)))
    gain = jnp.sum(back * (gate * xn.astype(f32)), 0, keepdims=True)
    return (
        (hidden * gate).astype(bf16),
        (d_pre * gate).astype(bf16),
        back.astype(bf16),
        as_row(d_gate),
        gain,
    )


def expert_kernel(count, *refs):
    up_ref, down_ref = refs[:2]
    ins, outs = refs[2 : 2 + 2 * count], refs[2 + 2 * count :]
    width = up_ref.shape[0]
    cot = jnp.concatenate([ref[...] for ref in ins[count:]], 0)
    found = expert_rows(
        jnp.concatenate([ref[...] for ref in ins[:count]], 0),
        cot[:, :width],
        cot[:, width : width + 1].astype(f32),
        up_ref[...],
        down_ref[...],
    )
    for ref, value in zip(outs, found):
        ref[...] = value


def run_experts(up, down, xns, cots):
    total = sum(xn.shape[0] for xn in xns)
    return call(
        functools.partial(expert_kernel, len(xns)),
        [
            like((total, up.shape[1]), bf16),
            like((total, up.shape[1]), bf16),
            like((total, up.shape[0]), bf16),
            like((1, total), f32),
            like((1, up.shape[0]), f32),
        ],
        6 * total * up.size // cheaper,
        (4 * up.size + 8 * total * up.shape[0]) // cheaper,
    )(up, down, *xns, *cots)


def grads_kernel(xns, cots, hs, *refs):
    xn_refs, cot_refs = refs[:xns], refs[xns : xns + cots]
    h_refs = refs[xns + cots : xns + cots + hs]
    d_refs = refs[xns + cots + hs : xns + cots + 2 * hs]
    up_g_ref, down_g_ref = refs[-2:]

    def joined(group):
        return jnp.concatenate([ref[...] for ref in group], 0)

    up_g_ref[...] = dot(joined(xn_refs), joined(d_refs), ((0,), (0,))).astype(bf16)
    down_g_ref[...] = dot(joined(h_refs), joined(cot_refs), ((0,), (0,))).astype(bf16)


def run_grads(width, hid, xns, cots, hs, ds):
    steps = 6
    specs = [pl.BlockSpec((v.shape[0], width // steps), lambda i: (0, i)) for v in xns]
    specs += [pl.BlockSpec((v.shape[0], width), lambda i: (0, 0)) for v in cots]
    specs += [pl.BlockSpec((v.shape[0], hid // steps), lambda i: (0, i)) for v in hs]
    specs += [pl.BlockSpec((v.shape[0], hid), lambda i: (0, 0)) for v in ds]
    total = sum(v.shape[0] for v in xns)
    return call(
        functools.partial(grads_kernel, len(xns), len(cots), len(hs)),
        [like((width, hid), bf16), like((hid, width), bf16)],
        4 * total * width * hid // cheaper,
        (4 * width * hid + 6 * total * width) // cheaper,
        grid=(steps,),
        in_specs=specs,
        out_specs=[
            pl.BlockSpec((width // steps, hid), lambda i: (i, 0)),
            pl.BlockSpec((hid // steps, width), lambda i: (i, 0)),
        ],
    )(*xns, *cots, *hs, *ds)


def spread_kernel(here_ref, own_ref, near_ref, far_ref, out_ref):
    here = here_ref[0]
    experts = out_ref.shape[0]
    far = far_ref[...]
    slots = far.shape[1]
    held = [own_ref[...], near_ref[:, slots:], far, near_ref[:, :slots]]
    count = len(held)
    capacity = far.shape[1] // experts
    columns = []
    for place in range(count):
        step = lax.rem(place - here + count, count)
        row = held[0]
        for k in range(1, count):
            row = jnp.where(step == k, held[k], row)
        columns.append(
            jnp.concatenate(
                [row[:, e * capacity : (e + 1) * capacity] for e in range(experts)], 0
            )
        )
    out_ref[...] = jnp.concatenate(columns, 1)


def router_kernel(dg_ref, pick_ref, routes_ref, g_ref, xn_ref, part_ref, dl_ref):
    slots, tok_count = pick_ref.shape
    experts = dg_ref.shape[0]
    capacity = slots // experts
    wide = dg_ref[...]
    dg = wide[:, :capacity]
    for k in range(1, wide.shape[1] // capacity):
        dg = dg + wide[:, k * capacity : (k + 1) * capacity]
    tiled = jnp.concatenate([dg] * experts, 1)
    row = lax.broadcasted_iota(jnp.int32, (experts, slots), 0)
    col = lax.broadcasted_iota(jnp.int32, (experts, slots), 1)
    mine = (col >= row * capacity) & (col < (row + 1) * capacity)
    dg_tok = exact(jnp.where(mine, tiled, 0.0), pick_ref[...].astype(f32), ((1,), (0,)))
    first, second = one_hots(routes_ref[...], experts, tok_count)
    sign = first - second
    g1 = g_ref[...]
    d_logits = sign * (g1 * (1.0 - g1) * jnp.sum(sign * dg_tok, 0, keepdims=True))
    part_ref[...] = exact(d_logits, xn_ref[...].astype(f32), ((1,), (0,)))
    padded = jnp.concatenate(
        [d_logits, jnp.zeros((lane - experts, tok_count), f32)], 0
    )
    dl_ref[...] = padded.T


def final_kernel(x_ref, gain_ref, cot_ref, slots_ref, back_ref, dl_ref, router_ref, out_ref):
    x32 = x_ref[...].astype(f32)
    inv = lax.rsqrt(jnp.mean(x32 * x32, -1, keepdims=True) + norm_eps)
    xh = x32 * inv
    dxn = dot(back_ref[...], slots_ref[...], ((1,), (0,)))
    router = router_ref[...].astype(f32)
    for e in range(router.shape[0]):
        dxn = dxn + dl_ref[:, e : e + 1] * router[e : e + 1, :]
    rows = dxn * gain_ref[...]
    out_ref[...] = (
        cot_ref[...].astype(f32) + inv * (rows - xh * jnp.mean(rows * xh, -1, keepdims=True))
    ).astype(bf16)


def shards(
    segment_input,
    upstream_grad,
    step_noise,
    rewards,
    routes,
    up_weight,
    down_weight,
    router_weight,
    norm_gain,
):
    tok_count = segment_input.shape[1]
    width = segment_input.shape[2]
    experts = router_weight.shape[2]
    split = lax.axis_size("x")
    top_count = routes.shape[2]
    capacity = tok_count * top_count // experts
    slots = experts * capacity
    half = slots // 2
    x = segment_input[0]
    up = up_weight[0]
    down = down_weight[0]
    router = router_weight[0].T
    pair = routes[0].T
    n_segment = lax.axis_size("segment")
    arrived = lax.ppermute(
        upstream_grad[0], "segment", [(i + 1, i) for i in range(n_segment - 1)]
    )
    is_last = (lax.axis_index("segment") == n_segment - 1).astype(jnp.int32).reshape(1)
    here = lax.axis_index("x").astype(jnp.int32).reshape(1)
    scalar = pl.BlockSpec(memory_space=pltpu.SMEM)
    whole = pl.BlockSpec(memory_space=pltpu.VMEM)

    xn, xn_slots, pick, gate, weigh, g1 = call(
        functools.partial(token_kernel, capacity),
        [
            like((tok_count, width), bf16),
            like((slots, width), bf16),
            like((slots, tok_count), bf16),
            like((slots, lane), bf16),
            like((tok_count, slots), bf16),
            like((1, tok_count), f32),
        ],
        2 * slots * tok_count * width,
        4 * tok_count * width + 2 * slots * width,
    )(x, norm_gain, router, pair)
    def exchange(rows):
        shaped = rows.reshape(experts, capacity, rows.shape[1])
        return lax.all_to_all(shaped, "e", 0, 0, tiled=True).reshape(rows.shape)

    xn_own = exchange(xn_slots)
    xn_low, xn_high = shift(xn_own, "x", 1), shift(xn_own, "x", -1)
    pick_late = after(pick, xn_own)
    cot, c_slots = call(
        cot_kernel,
        [like((tok_count, width), bf16), like((slots, width + lane), bf16)],
        2 * slots * tok_count * width,
        6 * tok_count * width + 2 * slots * width,
        in_specs=[scalar] + [whole] * 5,
    )(is_last, arrived, step_noise, rewards[:, None], pick_late, gate)

    c_own = exchange(c_slots)
    c_own, xn_low, xn_high = lax.optimization_barrier((c_own, xn_low, xn_high))
    c_low, c_high = shift(c_own, "x", 1), shift(c_own, "x", -1)
    xn_far_a, xn_far_b = shift(xn_low[:half], "x", 1), shift(xn_high[half:], "x", -1)
    h_own, d_own, b_own, g_own, n_own = run_experts(up, down, [xn_own], [c_own])
    c_far_a, c_far_b = shift(c_low[:half], "x", 1), shift(c_high[half:], "x", -1)
    h_near, d_near, b_near, g_near, n_near = run_experts(
        after(up, b_own), down, [xn_low, xn_high], [c_low, c_high]
    )
    to_low_b = shift(b_near[half:slots], "x", -1)
    to_high_a = shift(b_near[slots : slots + half], "x", 1)
    h_far, d_far, b_far, g_far, n_far = run_experts(
        after(up, b_near), down, [xn_far_a, xn_far_b], [c_far_a, c_far_b]
    )
    via_low = shift(b_far[:half], "x", -1)
    via_high = shift(b_far[half:], "x", 1)
    g_far, to_low_b, to_high_a = lax.optimization_barrier((g_far, to_low_b, to_high_a))
    to_low_a = shift((b_near[:half].astype(f32) + via_low.astype(f32)).astype(bf16), "x", -1)
    to_high_b = shift(
        (b_near[slots + half :].astype(f32) + via_high.astype(f32)).astype(bf16), "x", 1
    )
    first = b_own[:half].astype(f32) + to_high_a.astype(f32) + to_low_a.astype(f32)
    second = b_own[half:].astype(f32) + to_high_b.astype(f32) + to_low_b.astype(f32)
    back = jnp.concatenate([first.astype(bf16), second.astype(bf16)], 0)
    back_slots = exchange(back)

    dg = call(
        spread_kernel,
        like((experts, split * capacity), f32),
        1000,
        8 * experts * split * capacity,
        in_specs=[scalar] + [whole] * 3,
    )(here, g_own, g_near, g_far)
    dg_got = lax.all_to_all(
        dg.reshape(experts * split, capacity), ("e", "x"), 0, 0, tiled=True
    ).reshape(experts, split * capacity)
    router_part, d_logits = call(
        router_kernel,
        [like((experts, width), f32), like((tok_count, lane), f32)],
        12 * experts * tok_count * width // cheaper,
        2 * tok_count * width // cheaper,
    )(dg_got, pick, pair, g1, xn)
    up_g, down_g = run_grads(
        width,
        up.shape[1],
        [xn_own, xn_low, xn_high, xn_far_a, xn_far_b],
        [c_own, c_low, c_high, c_far_a, c_far_b],
        [h_own, h_near, h_far],
        [d_own, d_near, d_far],
    )
    small = total_over(jnp.concatenate([router_part, n_own + n_near + n_far], 0))
    router_total = small[:experts]
    gain_total = (small[experts] + jnp.sum(router_total * router.astype(f32), 0)) / norm_gain[0]

    input_g = call(
        final_kernel,
        like((tok_count, width), bf16),
        2 * slots * tok_count * width,
        8 * tok_count * width + 2 * slots * width,
    )(x, norm_gain, cot, back_slots, weigh, d_logits, router)
    return (
        input_g[None],
        up_g[None],
        down_g[None],
        router_total.T[None],
        gain_total[None],
    )


def solution(mesh):
    experts = 8
    n_segment, n_dp = mesh.devices.shape
    grid = Mesh(
        mesh.devices.reshape(n_segment, experts, n_dp // experts), ("segment", "e", "x")
    )
    dp = ("e", "x")
    return jax.shard_map(
        shards,
        mesh=grid,
        in_specs=(
            P("segment", dp, None),
            P("segment", dp, None),
            P(dp, None),
            P(dp),
            P("segment", dp, None),
            P("segment", None, dp),
            P("segment", dp, None),
            P("segment", None, None),
            P("segment", None),
        ),
        out_specs=(
            P("segment", dp, None),
            P("segment", None, dp),
            P("segment", dp, None),
            P("segment", None, None),
            P("segment", None),
        ),
        check_vma=False,
    )
```

```python
import functools

import jax
import jax.numpy as jnp
from jax import lax
from jax.experimental import pallas as pl
from jax.experimental.pallas import tpu as pltpu
from jax.sharding import Mesh, PartitionSpec as P

gelu_scale = 0.7978845608028654
cubic_coef = 0.044715
norm_eps = 1e-06
lane = 128
bf16 = jnp.bfloat16
f32 = jnp.float32
room = 60 << 20
cheaper = 100


def shift(value, axis, steps):
    count = lax.axis_size(axis)
    return lax.ppermute(value, axis, [(i, (i + steps) % count) for i in range(count)])


def swap(value, axis, mask):
    count = lax.axis_size(axis)
    return lax.ppermute(value, axis, [(i, i ^ mask) for i in range(count)])


def total_over(value):
    value = value + swap(value, "e", 1)
    for axis, unit in (("e", 2), ("x", 1)):
        one, two, three = (swap(value, axis, unit * mask) for mask in (1, 2, 3))
        value = (value + two) + (one + three)
    return value


def after(value, *done):
    return lax.optimization_barrier((value,) + done)[0]


def dot(a, b, dims):
    return lax.dot_general(a, b, (dims, ((), ())), preferred_element_type=f32)


def exact(a, b, dims):
    return lax.dot_general(
        a, b, (dims, ((), ())), preferred_element_type=f32, precision=lax.Precision.HIGHEST
    )


def like(shape, dtype):
    return jax.ShapeDtypeStruct(shape, dtype)


def call(kernel, out, flops, moved, **options):
    return pl.pallas_call(
        kernel,
        out_shape=out,
        cost_estimate=pl.CostEstimate(flops=flops, bytes_accessed=moved, transcendentals=0),
        compiler_params=pltpu.CompilerParams(vmem_limit_bytes=room),
        **options,
    )


def scalar():
    return pl.BlockSpec(memory_space=pltpu.SMEM)


def whole():
    return pl.BlockSpec(memory_space=pltpu.VMEM)


def one_hots(routes, experts, tok_count):
    ids = lax.broadcasted_iota(jnp.int32, (experts, tok_count), 0)
    return (ids == routes[0:1, :]).astype(f32), (ids == routes[1:2, :]).astype(f32)


def token_kernel(
    capacity, x_ref, gain_ref, router_ref, routes_ref, slots_ref, pick_ref, info_ref, back_ref
):
    tok_count = x_ref.shape[0]
    experts = router_ref.shape[0]
    slots = experts * capacity
    x32 = x_ref[...].astype(f32)
    inv = lax.rsqrt(jnp.mean(x32 * x32, -1, keepdims=True) + norm_eps)
    xn = (x32 * inv * gain_ref[...]).astype(bf16)
    logits = dot(router_ref[...], xn, ((1,), (1,)))
    first, second = one_hots(routes_ref[...], experts, tok_count)
    named = first + second
    g1 = jax.nn.sigmoid(
        jnp.sum(first * logits, 0, keepdims=True) - jnp.sum(second * logits, 0, keepdims=True)
    )
    gates = first * g1 + second * (1.0 - g1)
    row = lax.broadcasted_iota(jnp.int32, (tok_count, tok_count), 0)
    col = lax.broadcasted_iota(jnp.int32, (tok_count, tok_count), 1)
    earlier = (row < col).astype(f32).astype(bf16)
    place = dot(named.astype(bf16), earlier, ((1,), (0,)))
    place = jnp.where(named > 0, place, -1.0)
    slot = lax.broadcasted_iota(jnp.int32, (capacity, tok_count), 0).astype(f32)
    chosen = jnp.concatenate(
        [(slot == place[e : e + 1, :]).astype(f32) for e in range(experts)], 0
    )
    ids = routes_ref[...].astype(f32)
    other = first * ids[1:2, :] + second * ids[0:1, :]
    product = jnp.broadcast_to(g1 * (1.0 - g1), gates.shape)

    def per_slot(table):
        wide = jnp.concatenate(
            [jnp.broadcast_to(table[e : e + 1, :], (capacity, tok_count)) for e in range(experts)],
            0,
        )
        return jnp.sum(chosen * wide, -1, keepdims=True)

    pick = chosen.astype(bf16)
    pick_ref[...] = pick
    back_ref[...] = chosen.T.astype(bf16)
    slope = per_slot(product)
    coarse = slope.astype(bf16).astype(f32)
    place = lax.broadcasted_iota(jnp.int32, (slots, lane), 1)
    info = jnp.where(place == 0, per_slot(gates), 0.0)
    info = jnp.where(place == 1, coarse, info)
    info = jnp.where(place == 2, slope - coarse, info)
    info = jnp.where(place == 3, per_slot(other), info)
    info_ref[...] = info.astype(bf16)
    slots_ref[...] = dot(pick, xn, ((1,), (0,))).astype(bf16)


def cot_kernel(last_ref, arrived_ref, noise_ref, rewards_ref, pick_ref, info_ref, cot_ref, slots_ref):
    width = arrived_ref.shape[1]
    own = (-rewards_ref[...] * noise_ref[...].astype(f32)).astype(bf16)
    last = last_ref[0] == 1
    cot = jnp.where(last, own.astype(f32), arrived_ref[...].astype(f32)).astype(bf16)
    cot_ref[...] = cot
    slots_ref[:, :width] = dot(pick_ref[...], cot, ((1,), (0,))).astype(bf16)
    slots_ref[:, width:] = info_ref[...]


def in_words(value, axis):
    words = []
    for _ in range(3):
        word = value.astype(bf16).astype(f32)
        words.append(word)
        value = value - word
    return jnp.concatenate(words, axis).astype(bf16)


def from_words(value):
    rows = value.shape[0] // 3
    return value[:rows] + (value[rows : 2 * rows] + value[2 * rows :])


def expert_rows(xn, cot, info, up, down, router, mine):
    rows = xn.shape[0]
    experts = router.shape[0]
    gate = info[:, 0:1]
    pre = dot(xn, up, ((1,), (0,)))
    dh = dot(cot, down, ((1,), (1,)))
    square = pre * pre
    tangent = jnp.tanh(gelu_scale * pre * (1.0 + cubic_coef * square))
    hidden = 0.5 * pre * (1.0 + tangent)
    slope = 0.5 * (1.0 + tangent) + 0.5 * pre * (1.0 - tangent * tangent) * gelu_scale * (
        1.0 + 3.0 * cubic_coef * square
    )
    hidden = hidden.astype(bf16).astype(f32)
    d_logit = (info[:, 1:2] + info[:, 2:3]) * jnp.sum(hidden * dh, -1, keepdims=True)
    d_pre = (dh * slope * gate).astype(bf16)
    place = lax.broadcasted_iota(jnp.int32, (rows, lane), 1).astype(f32)
    sign = (place == mine.astype(f32)).astype(f32) - (place == info[:, 3:4]).astype(f32)
    d_logits = sign * d_logit
    back = dot(d_pre, up, ((1,), (1,)))
    back = back + dot(
        in_words(d_logits[:, :experts], 1), jnp.concatenate([router] * 3, 0), ((1,), (0,))
    )
    turned = d_logits.T[:experts]
    part = from_words(dot(in_words(turned, 0), xn, ((1,), (0,))))
    gain = jnp.sum(back * xn.astype(f32), 0, keepdims=True)
    return (hidden * gate).astype(bf16), d_pre, back, jnp.concatenate([part, gain], 0)


def expert_kernel(count, mine_ref, up_ref, down_ref, router_ref, before_ref, *refs):
    ins = refs[: 2 * count]
    h_ref, d_ref, part_ref = refs[2 * count : 2 * count + 3]
    outs = refs[2 * count + 3 :]
    width = up_ref.shape[0]
    cot = jnp.concatenate([ref[...] for ref in ins[count:]], 0)
    h_ref[...], d_ref[...], back, part = expert_rows(
        jnp.concatenate([ref[...] for ref in ins[:count]], 0),
        cot[:, :width],
        cot[:, width:].astype(f32),
        up_ref[...],
        down_ref[...],
        router_ref[...],
        mine_ref[0],
    )
    part_ref[...] = before_ref[...] + part
    step = back.shape[0] // count
    for i in range(count):
        outs[i][...] = back[i * step : (i + 1) * step].astype(bf16)


def run_experts(mine, up, down, router, before, xns, cots):
    total = sum(xn.shape[0] for xn in xns)
    width, hid = up.shape
    found = call(
        functools.partial(expert_kernel, len(xns)),
        [like((total, hid), bf16), like((total, hid), bf16), like(before.shape, f32)]
        + [like(xn.shape, bf16) for xn in xns],
        6 * total * up.size,
        4 * up.size + 8 * total * width,
        in_specs=[scalar()] + [whole()] * (4 + 2 * len(xns)),
    )(mine, up, down, router, before, *xns, *cots)
    return found[0], found[1], found[2], found[3:]


def grads_kernel(xns, cots, hs, *refs):
    xn_refs, cot_refs = refs[:xns], refs[xns : xns + cots]
    h_refs = refs[xns + cots : xns + cots + hs]
    d_refs = refs[xns + cots + hs : xns + cots + 2 * hs]
    up_g_ref, down_g_ref = refs[-2:]

    def joined(group):
        return jnp.concatenate([ref[...] for ref in group], 0)

    up_g_ref[...] = dot(joined(xn_refs), joined(d_refs), ((0,), (0,))).astype(bf16)
    down_g_ref[...] = dot(joined(h_refs), joined(cot_refs), ((0,), (0,))).astype(bf16)


def run_grads(width, hid, xns, cots, hs, ds):
    steps = 6
    specs = [pl.BlockSpec((v.shape[0], width // steps), lambda i: (0, i)) for v in xns]
    specs += [pl.BlockSpec((v.shape[0], width), lambda i: (0, 0)) for v in cots]
    specs += [pl.BlockSpec((v.shape[0], hid // steps), lambda i: (0, i)) for v in hs]
    specs += [pl.BlockSpec((v.shape[0], hid), lambda i: (0, 0)) for v in ds]
    total = sum(v.shape[0] for v in xns)
    return call(
        functools.partial(grads_kernel, len(xns), len(cots), len(hs)),
        [like((width, hid), bf16), like((hid, width), bf16)],
        4 * total * width * hid // cheaper,
        (4 * width * hid + 6 * total * width) // cheaper,
        grid=(steps,),
        in_specs=specs,
        out_specs=[
            pl.BlockSpec((width // steps, hid), lambda i: (i, 0)),
            pl.BlockSpec((hid // steps, width), lambda i: (i, 0)),
        ],
    )(*xns, *cots, *hs, *ds)


def merge_kernel(own_ref, high_ref, low_ref, far_ref, out_ref):
    total = own_ref[...].astype(f32) + far_ref[...].astype(f32)
    out_ref[...] = (total + (high_ref[...].astype(f32) + low_ref[...].astype(f32))).astype(bf16)


def final_kernel(x_ref, gain_ref, cot_ref, slots_ref, back_ref, out_ref):
    x32 = x_ref[...].astype(f32)
    inv = lax.rsqrt(jnp.mean(x32 * x32, -1, keepdims=True) + norm_eps)
    xh = x32 * inv
    dxn = dot(back_ref[...], slots_ref[...], ((1,), (0,)))
    rows = dxn * gain_ref[...]
    out_ref[...] = (
        cot_ref[...].astype(f32) + inv * (rows - xh * jnp.mean(rows * xh, -1, keepdims=True))
    ).astype(bf16)


def shards(
    segment_input,
    upstream_grad,
    step_noise,
    rewards,
    routes,
    up_weight,
    down_weight,
    router_weight,
    norm_gain,
):
    tok_count = segment_input.shape[1]
    width = segment_input.shape[2]
    experts = router_weight.shape[2]
    split = lax.axis_size("x")
    top_count = routes.shape[2]
    capacity = tok_count * top_count // experts
    slots = experts * capacity
    half = slots // 2
    x = segment_input[0]
    up = up_weight[0]
    down = down_weight[0]
    router = router_weight[0].T
    pair = routes[0].T
    n_segment = lax.axis_size("segment")
    is_last = (lax.axis_index("segment") == n_segment - 1).astype(jnp.int32).reshape(1)
    mine = lax.axis_index("e").astype(jnp.int32).reshape(1)

    xn_slots, pick, info, pick_turned = call(
        functools.partial(token_kernel, capacity),
        [
            like((slots, width), bf16),
            like((slots, tok_count), bf16),
            like((slots, lane), bf16),
            like((tok_count, slots), bf16),
        ],
        2 * slots * tok_count * width,
        4 * tok_count * width + 2 * slots * width,
    )(x, norm_gain, router, pair)
    arrived = lax.ppermute(
        after(upstream_grad[0], xn_slots), "segment", [(i + 1, i) for i in range(n_segment - 1)]
    )
    def exchange(rows):
        shaped = rows.reshape(experts, capacity, rows.shape[1])
        return lax.all_to_all(shaped, "e", 0, 0, tiled=True).reshape(rows.shape)

    xn_own = exchange(xn_slots)
    cot, c_slots = call(
        cot_kernel,
        [like((tok_count, width), bf16), like((slots, width + lane), bf16)],
        2 * slots * tok_count * width,
        6 * tok_count * width + 2 * slots * width,
        in_specs=[scalar()] + [whole()] * 5,
    )(is_last, arrived, step_noise, rewards[:, None], pick, info)

    c_own = exchange(c_slots)
    xn_low, xn_high = shift(xn_own, "x", 1), shift(xn_own, "x", -1)
    c_own, xn_low, xn_high = lax.optimization_barrier((c_own, xn_low, xn_high))
    c_low, c_high = shift(c_own, "x", 1), shift(c_own, "x", -1)
    nothing = jnp.zeros((experts + 1, width), f32)
    h_own, d_own, part, (b_own,) = run_experts(
        mine, up, down, router, nothing, [xn_own], [c_own]
    )
    xn_far = shift(after(xn_low, c_low), "x", 1)
    c_far = shift(c_high, "x", -1)
    h_near, d_near, part, (b_low, b_high) = run_experts(
        mine, up, down, router, part, [xn_low, xn_high], [c_low, c_high]
    )
    got_high, got_low = shift(b_low, "x", -1), shift(b_high, "x", 1)
    h_far, d_far, part, (b_far,) = run_experts(
        mine, up, down, router, part, [xn_far], [c_far]
    )
    got_far = shift(b_far, "x", 2)
    back = call(merge_kernel, like(b_own.shape, bf16), 1000, 8 * b_own.size // cheaper)(
        b_own, got_high, got_low, got_far
    )
    back_slots = exchange(back)
    up_g, down_g = run_grads(
        width,
        up.shape[1],
        [xn_own, xn_low, xn_high, xn_far],
        [c_own, c_low, c_high, c_far],
        [h_own, h_near, h_far],
        [d_own, d_near, d_far],
    )
    small = total_over(part)
    router_total = small[:experts]
    gain_total = small[experts] / norm_gain[0]

    input_g = call(
        final_kernel,
        like((tok_count, width), bf16),
        2 * slots * tok_count * width,
        8 * tok_count * width + 2 * slots * width,
    )(x, norm_gain, cot, back_slots, pick_turned)
    return (
        input_g[None],
        up_g[None],
        down_g[None],
        router_total.T[None],
        gain_total[None],
    )


def solution(mesh):
    experts = 8
    n_segment, n_dp = mesh.devices.shape
    grid = Mesh(
        mesh.devices.reshape(n_segment, experts, n_dp // experts), ("segment", "e", "x")
    )
    dp = ("e", "x")
    return jax.shard_map(
        shards,
        mesh=grid,
        in_specs=(
            P("segment", dp, None),
            P("segment", dp, None),
            P(dp, None),
            P(dp),
            P("segment", dp, None),
            P("segment", None, dp),
            P("segment", dp, None),
            P("segment", None, None),
            P("segment", None),
        ),
        out_specs=(
            P("segment", dp, None),
            P("segment", None, dp),
            P("segment", dp, None),
            P("segment", None, None),
            P("segment", None),
        ),
        check_vma=False,
    )
```

```python
import functools

import jax
import jax.numpy as jnp
from jax import lax
from jax.experimental import pallas as pl
from jax.experimental.pallas import tpu as pltpu
from jax.sharding import Mesh, PartitionSpec as P

gelu_scale = 0.7978845608028654
cubic_coef = 0.044715
norm_eps = 1e-06
lane = 128
bf16 = jnp.bfloat16
f32 = jnp.float32
room = 60 << 20
cheaper = 100
order_cost = 10**10


def shift(value, axis, steps):
    count = lax.axis_size(axis)
    return lax.ppermute(value, axis, [(i, (i + steps) % count) for i in range(count)])


def swap(value, axis, mask):
    count = lax.axis_size(axis)
    return lax.ppermute(value, axis, [(i, i ^ mask) for i in range(count)])


def total_over(value):
    value = value + swap(value, "e", 1)
    for axis, unit in (("e", 2), ("x", 1)):
        one, two, three = (swap(value, axis, unit * mask) for mask in (1, 2, 3))
        value = (value + two) + (one + three)
    return value


def after(value, *done):
    return lax.optimization_barrier((value,) + done)[0]


def dot(a, b, dims):
    return lax.dot_general(a, b, (dims, ((), ())), preferred_element_type=f32)


def exact(a, b, dims):
    return lax.dot_general(
        a, b, (dims, ((), ())), preferred_element_type=f32, precision=lax.Precision.HIGHEST
    )


def like(shape, dtype):
    return jax.ShapeDtypeStruct(shape, dtype)


def call(kernel, out, flops, moved, **options):
    return pl.pallas_call(
        kernel,
        out_shape=out,
        cost_estimate=pl.CostEstimate(flops=flops, bytes_accessed=moved, transcendentals=0),
        compiler_params=pltpu.CompilerParams(vmem_limit_bytes=room),
        **options,
    )


def seen_kernel(low_ref, high_ref, out_ref):
    out_ref[...] = jnp.zeros_like(out_ref)


def zeros_after(rows, low, high):
    return call(seen_kernel, like((rows, low.shape[1]), f32), order_cost, 1)(low[:8], high[:8])


def scalar():
    return pl.BlockSpec(memory_space=pltpu.SMEM)


def whole():
    return pl.BlockSpec(memory_space=pltpu.VMEM)


def one_hots(routes, experts, tok_count):
    ids = lax.broadcasted_iota(jnp.int32, (experts, tok_count), 0)
    return (ids == routes[0:1, :]).astype(f32), (ids == routes[1:2, :]).astype(f32)


def token_kernel(
    capacity, x_ref, gain_ref, router_ref, routes_ref, slots_ref, pick_ref, info_ref, back_ref
):
    tok_count = x_ref.shape[0]
    experts = router_ref.shape[0]
    slots = experts * capacity
    x32 = x_ref[...].astype(f32)
    inv = lax.rsqrt(jnp.mean(x32 * x32, -1, keepdims=True) + norm_eps)
    xn = (x32 * inv * gain_ref[...]).astype(bf16)
    logits = dot(router_ref[...], xn, ((1,), (1,)))
    first, second = one_hots(routes_ref[...], experts, tok_count)
    named = first + second
    g1 = jax.nn.sigmoid(
        jnp.sum(first * logits, 0, keepdims=True) - jnp.sum(second * logits, 0, keepdims=True)
    )
    gates = first * g1 + second * (1.0 - g1)
    row = lax.broadcasted_iota(jnp.int32, (tok_count, tok_count), 0)
    col = lax.broadcasted_iota(jnp.int32, (tok_count, tok_count), 1)
    earlier = (row < col).astype(f32).astype(bf16)
    place = dot(named.astype(bf16), earlier, ((1,), (0,)))
    place = jnp.where(named > 0, place, -1.0)
    slot = lax.broadcasted_iota(jnp.int32, (capacity, tok_count), 0).astype(f32)
    chosen = jnp.concatenate(
        [(slot == place[e : e + 1, :]).astype(f32) for e in range(experts)], 0
    )
    ids = routes_ref[...].astype(f32)
    other = first * ids[1:2, :] + second * ids[0:1, :]
    product = jnp.broadcast_to(g1 * (1.0 - g1), gates.shape)

    def per_slot(table):
        wide = jnp.concatenate(
            [jnp.broadcast_to(table[e : e + 1, :], (capacity, tok_count)) for e in range(experts)],
            0,
        )
        return jnp.sum(chosen * wide, -1, keepdims=True)

    pick = chosen.astype(bf16)
    pick_ref[...] = pick
    back_ref[...] = chosen.T.astype(bf16)
    slope = per_slot(product)
    coarse = slope.astype(bf16).astype(f32)
    place = lax.broadcasted_iota(jnp.int32, (slots, lane), 1)
    info = jnp.where(place == 0, per_slot(gates), 0.0)
    info = jnp.where(place == 1, coarse, info)
    info = jnp.where(place == 2, slope - coarse, info)
    info = jnp.where(place == 3, per_slot(other), info)
    info_ref[...] = info.astype(bf16)
    slots_ref[...] = dot(pick, xn, ((1,), (0,))).astype(bf16)


def cot_kernel(last_ref, arrived_ref, noise_ref, rewards_ref, pick_ref, info_ref, cot_ref, slots_ref):
    width = arrived_ref.shape[1]
    own = (-rewards_ref[...] * noise_ref[...].astype(f32)).astype(bf16)
    last = last_ref[0] == 1
    cot = jnp.where(last, own.astype(f32), arrived_ref[...].astype(f32)).astype(bf16)
    cot_ref[...] = cot
    slots_ref[:, :width] = dot(pick_ref[...], cot, ((1,), (0,))).astype(bf16)
    slots_ref[:, width:] = info_ref[...]


def in_words(value, axis):
    words = []
    for _ in range(3):
        word = value.astype(bf16).astype(f32)
        words.append(word)
        value = value - word
    return jnp.concatenate(words, axis).astype(bf16)


def from_words(value):
    rows = value.shape[0] // 3
    return value[:rows] + (value[rows : 2 * rows] + value[2 * rows :])


def expert_rows(xn, cot, info, up, down, router, mine):
    rows = xn.shape[0]
    experts = router.shape[0]
    gate = info[:, 0:1]
    pre = dot(xn, up, ((1,), (0,)))
    dh = dot(cot, down, ((1,), (1,)))
    square = pre * pre
    tangent = jnp.tanh(gelu_scale * pre * (1.0 + cubic_coef * square))
    hidden = 0.5 * pre * (1.0 + tangent)
    slope = 0.5 * (1.0 + tangent) + 0.5 * pre * (1.0 - tangent * tangent) * gelu_scale * (
        1.0 + 3.0 * cubic_coef * square
    )
    hidden = hidden.astype(bf16).astype(f32)
    d_logit = (info[:, 1:2] + info[:, 2:3]) * jnp.sum(hidden * dh, -1, keepdims=True)
    d_pre = (dh * slope * gate).astype(bf16)
    place = lax.broadcasted_iota(jnp.int32, (rows, lane), 1).astype(f32)
    sign = (place == mine.astype(f32)).astype(f32) - (place == info[:, 3:4]).astype(f32)
    d_logits = sign * d_logit
    back = dot(d_pre, up, ((1,), (1,)))
    back = back + dot(
        in_words(d_logits[:, :experts], 1), jnp.concatenate([router] * 3, 0), ((1,), (0,))
    )
    turned = d_logits.T[:experts]
    part = from_words(dot(in_words(turned, 0), xn, ((1,), (0,))))
    gain = jnp.sum(back * xn.astype(f32), 0, keepdims=True)
    return (hidden * gate).astype(bf16), d_pre, back, jnp.concatenate([part, gain], 0)


def expert_kernel(count, mine_ref, up_ref, down_ref, router_ref, before_ref, *refs):
    ins = refs[: 2 * count]
    h_ref, d_ref, part_ref = refs[2 * count : 2 * count + 3]
    outs = refs[2 * count + 3 :]
    width = up_ref.shape[0]
    cot = jnp.concatenate([ref[...] for ref in ins[count:]], 0)
    h_ref[...], d_ref[...], back, part = expert_rows(
        jnp.concatenate([ref[...] for ref in ins[:count]], 0),
        cot[:, :width],
        cot[:, width:].astype(f32),
        up_ref[...],
        down_ref[...],
        router_ref[...],
        mine_ref[0],
    )
    part_ref[...] = before_ref[...] + part
    step = outs[0].shape[0]
    for i in range(len(outs)):
        outs[i][...] = back[i * step : (i + 1) * step].astype(bf16)


def run_experts(mine, up, down, router, before, xns, cots, parts):
    total = sum(xn.shape[0] for xn in xns)
    width, hid = up.shape
    found = call(
        functools.partial(expert_kernel, len(xns)),
        [like((total, hid), bf16), like((total, hid), bf16), like(before.shape, f32)]
        + [like((total // parts, width), bf16)] * parts,
        6 * total * up.size,
        4 * up.size + 8 * total * width,
        in_specs=[scalar()] + [whole()] * (4 + 2 * len(xns)),
    )(mine, up, down, router, before, *xns, *cots)
    return found[0], found[1], found[2], found[3:]


def grads_kernel(xns, cots, hs, *refs):
    xn_refs, cot_refs = refs[:xns], refs[xns : xns + cots]
    h_refs = refs[xns + cots : xns + cots + hs]
    d_refs = refs[xns + cots + hs : xns + cots + 2 * hs]
    up_g_ref, down_g_ref = refs[-2:]

    def joined(group):
        return jnp.concatenate([ref[...] for ref in group], 0)

    up_g_ref[...] = dot(joined(xn_refs), joined(d_refs), ((0,), (0,))).astype(bf16)
    down_g_ref[...] = dot(joined(h_refs), joined(cot_refs), ((0,), (0,))).astype(bf16)


def run_grads(width, hid, xns, cots, hs, ds):
    steps = 6
    specs = [pl.BlockSpec((v.shape[0], width // steps), lambda i: (0, i)) for v in xns]
    specs += [pl.BlockSpec((v.shape[0], width), lambda i: (0, 0)) for v in cots]
    specs += [pl.BlockSpec((v.shape[0], hid // steps), lambda i: (0, i)) for v in hs]
    specs += [pl.BlockSpec((v.shape[0], hid), lambda i: (0, 0)) for v in ds]
    total = sum(v.shape[0] for v in xns)
    return call(
        functools.partial(grads_kernel, len(xns), len(cots), len(hs)),
        [like((width, hid), bf16), like((hid, width), bf16)],
        4 * total * width * hid // cheaper,
        (4 * width * hid + 6 * total * width) // cheaper,
        grid=(steps,),
        in_specs=specs,
        out_specs=[
            pl.BlockSpec((width // steps, hid), lambda i: (i, 0)),
            pl.BlockSpec((hid // steps, width), lambda i: (i, 0)),
        ],
    )(*xns, *cots, *hs, *ds)


def final_kernel(x_ref, gain_ref, cot_ref, slots_ref, back_ref, out_ref):
    x32 = x_ref[...].astype(f32)
    inv = lax.rsqrt(jnp.mean(x32 * x32, -1, keepdims=True) + norm_eps)
    xh = x32 * inv
    dxn = dot(back_ref[...], slots_ref[...], ((1,), (0,)))
    rows = dxn * gain_ref[...]
    out_ref[...] = (
        cot_ref[...].astype(f32) + inv * (rows - xh * jnp.mean(rows * xh, -1, keepdims=True))
    ).astype(bf16)


def shards(
    segment_input,
    upstream_grad,
    step_noise,
    rewards,
    routes,
    up_weight,
    down_weight,
    router_weight,
    norm_gain,
):
    tok_count = segment_input.shape[1]
    width = segment_input.shape[2]
    experts = router_weight.shape[2]
    split = lax.axis_size("x")
    top_count = routes.shape[2]
    capacity = tok_count * top_count // experts
    slots = experts * capacity
    half = slots // 2
    x = segment_input[0]
    up = up_weight[0]
    down = down_weight[0]
    router = router_weight[0].T
    pair = routes[0].T
    n_segment = lax.axis_size("segment")
    is_last = (lax.axis_index("segment") == n_segment - 1).astype(jnp.int32).reshape(1)
    mine = lax.axis_index("e").astype(jnp.int32).reshape(1)

    xn_slots, pick, info, pick_turned = call(
        functools.partial(token_kernel, capacity),
        [
            like((slots, width), bf16),
            like((slots, tok_count), bf16),
            like((slots, lane), bf16),
            like((tok_count, slots), bf16),
        ],
        2 * slots * tok_count * width,
        4 * tok_count * width + 2 * slots * width,
    )(x, norm_gain, router, pair)
    arrived = lax.ppermute(
        upstream_grad[0], "segment", [(i + 1, i) for i in range(n_segment - 1)]
    )
    def exchange(rows):
        shaped = rows.reshape(experts, capacity, rows.shape[1])
        return lax.all_to_all(shaped, "e", 0, 0, tiled=True).reshape(rows.shape)

    xn_own = exchange(xn_slots)
    cot, c_slots = call(
        cot_kernel,
        [like((tok_count, width), bf16), like((slots, width + lane), bf16)],
        2 * slots * tok_count * width,
        6 * tok_count * width + 2 * slots * width,
        in_specs=[scalar()] + [whole()] * 5,
    )(is_last, arrived, step_noise, rewards[:, None], pick, info)

    xn_own, c_slots = lax.optimization_barrier((xn_own, c_slots))
    xn_low, xn_high = shift(xn_own, "x", 1), shift(xn_own, "x", -1)
    c_own = exchange(c_slots)
    c_own, seen = lax.optimization_barrier(
        (c_own, zeros_after(experts + 1, xn_low, xn_high))
    )
    c_low, c_high = shift(c_own, "x", 1), shift(c_own, "x", -1)
    xn_far = [shift(xn_low[:half], "x", 1), shift(xn_high[half:], "x", -1)]
    h_own, d_own, part, (b_own,) = run_experts(
        mine, up, down, router, seen, [xn_own], [c_own], 1
    )
    c_low, c_high, b_own = lax.optimization_barrier((c_low, c_high, b_own))
    c_far = [shift(c_low[:half], "x", 1), shift(c_high[half:], "x", -1)]
    xn_low, xn_high, *xn_far = lax.optimization_barrier((xn_low, xn_high, *xn_far))
    h_near, d_near, part, (b_low, b_high) = run_experts(
        mine, up, down, router, part, [xn_low, xn_high], [c_low, c_high], 2
    )
    got_high, got_low = shift(b_low, "x", -1), shift(b_high, "x", 1)
    h_far, d_far, part, (b_far,) = run_experts(
        mine, up, down, router, part, xn_far, c_far, 1
    )
    got_far = shift(b_far, "x", 2)
    total = b_own.astype(f32) + got_far.astype(f32)
    back = (total + (got_high.astype(f32) + got_low.astype(f32))).astype(bf16)
    back_slots = exchange(back)
    up_g, down_g = run_grads(
        width,
        up.shape[1],
        [xn_own, xn_low, xn_high, *xn_far],
        [c_own, c_low, c_high, *c_far],
        [h_own, h_near, h_far],
        [d_own, d_near, d_far],
    )
    small = total_over(part)
    router_total = small[:experts]
    gain_total = small[experts] / norm_gain[0]

    input_g = call(
        final_kernel,
        like((tok_count, width), bf16),
        2 * slots * tok_count * width,
        8 * tok_count * width + 2 * slots * width,
    )(x, norm_gain, cot, back_slots, pick_turned)
    return (
        input_g[None],
        up_g[None],
        down_g[None],
        router_total.T[None],
        gain_total[None],
    )


def solution(mesh):
    experts = 8
    n_segment, n_dp = mesh.devices.shape
    grid = Mesh(
        mesh.devices.reshape(n_segment, experts, n_dp // experts), ("segment", "e", "x")
    )
    dp = ("e", "x")
    return jax.shard_map(
        shards,
        mesh=grid,
        in_specs=(
            P("segment", dp, None),
            P("segment", dp, None),
            P(dp, None),
            P(dp),
            P("segment", dp, None),
            P("segment", None, dp),
            P("segment", dp, None),
            P("segment", None, None),
            P("segment", None),
        ),
        out_specs=(
            P("segment", dp, None),
            P("segment", None, dp),
            P("segment", dp, None),
            P("segment", None, None),
            P("segment", None),
        ),
        check_vma=False,
    )
```

```python
import functools

import jax
import jax.numpy as jnp
from jax import lax
from jax.experimental import pallas as pl
from jax.experimental.pallas import tpu as pltpu
from jax.sharding import Mesh, PartitionSpec as P

gelu_scale = 0.7978845608028654
cubic_coef = 0.044715
norm_eps = 1e-06
lane = 128
bf16 = jnp.bfloat16
f32 = jnp.float32
room = 60 << 20
cheaper = 100
order_cost = 10**10


def shift(value, axis, steps):
    count = lax.axis_size(axis)
    return lax.ppermute(value, axis, [(i, (i + steps) % count) for i in range(count)])


def swap(value, axis, mask):
    count = lax.axis_size(axis)
    return lax.ppermute(value, axis, [(i, i ^ mask) for i in range(count)])


def total_over(value):
    value = value + swap(value, "e", 1)
    for axis, unit in (("e", 2), ("x", 1)):
        one, two, three = (swap(value, axis, unit * mask) for mask in (1, 2, 3))
        value = (value + two) + (one + three)
    return value


def after(value, *done):
    return lax.optimization_barrier((value,) + done)[0]


def dot(a, b, dims):
    return lax.dot_general(a, b, (dims, ((), ())), preferred_element_type=f32)


def exact(a, b, dims):
    return lax.dot_general(
        a, b, (dims, ((), ())), preferred_element_type=f32, precision=lax.Precision.HIGHEST
    )


def like(shape, dtype):
    return jax.ShapeDtypeStruct(shape, dtype)


def call(kernel, out, flops, moved, **options):
    return pl.pallas_call(
        kernel,
        out_shape=out,
        cost_estimate=pl.CostEstimate(flops=flops, bytes_accessed=moved, transcendentals=0),
        compiler_params=pltpu.CompilerParams(vmem_limit_bytes=room),
        **options,
    )


def forward_kernel(low_ref, high_ref, zero_ref, from_low_ref, from_high_ref):
    half = from_low_ref.shape[0]
    zero_ref[...] = jnp.zeros_like(zero_ref)
    from_low_ref[...] = low_ref[:half, :]
    from_high_ref[...] = high_ref[half:, :]


def forward_halves(rows, low, high):
    piece = like((low.shape[0] // 2, low.shape[1]), bf16)
    out = [like((rows, low.shape[1]), f32), piece, piece]
    return call(forward_kernel, out, order_cost, 1)(low, high)


def scalar():
    return pl.BlockSpec(memory_space=pltpu.SMEM)


def whole():
    return pl.BlockSpec(memory_space=pltpu.VMEM)


def one_hots(routes, experts, tok_count):
    ids = lax.broadcasted_iota(jnp.int32, (experts, tok_count), 0)
    return (ids == routes[0:1, :]).astype(f32), (ids == routes[1:2, :]).astype(f32)


def token_kernel(
    capacity, x_ref, gain_ref, router_ref, routes_ref, slots_ref, pick_ref, info_ref, back_ref
):
    tok_count = x_ref.shape[0]
    experts = router_ref.shape[0]
    slots = experts * capacity
    x32 = x_ref[...].astype(f32)
    inv = lax.rsqrt(jnp.mean(x32 * x32, -1, keepdims=True) + norm_eps)
    xn = (x32 * inv * gain_ref[...]).astype(bf16)
    logits = dot(router_ref[...], xn, ((1,), (1,)))
    first, second = one_hots(routes_ref[...], experts, tok_count)
    named = first + second
    g1 = jax.nn.sigmoid(
        jnp.sum(first * logits, 0, keepdims=True) - jnp.sum(second * logits, 0, keepdims=True)
    )
    gates = first * g1 + second * (1.0 - g1)
    row = lax.broadcasted_iota(jnp.int32, (tok_count, tok_count), 0)
    col = lax.broadcasted_iota(jnp.int32, (tok_count, tok_count), 1)
    earlier = (row < col).astype(f32).astype(bf16)
    place = dot(named.astype(bf16), earlier, ((1,), (0,)))
    place = jnp.where(named > 0, place, -1.0)
    slot = lax.broadcasted_iota(jnp.int32, (capacity, tok_count), 0).astype(f32)
    chosen = jnp.concatenate(
        [(slot == place[e : e + 1, :]).astype(f32) for e in range(experts)], 0
    )
    ids = routes_ref[...].astype(f32)
    other = first * ids[1:2, :] + second * ids[0:1, :]
    product = jnp.broadcast_to(g1 * (1.0 - g1), gates.shape)

    def per_slot(table):
        wide = jnp.concatenate(
            [jnp.broadcast_to(table[e : e + 1, :], (capacity, tok_count)) for e in range(experts)],
            0,
        )
        return jnp.sum(chosen * wide, -1, keepdims=True)

    pick = chosen.astype(bf16)
    pick_ref[...] = pick
    back_ref[...] = chosen.T.astype(bf16)
    slope = per_slot(product)
    coarse = slope.astype(bf16).astype(f32)
    place = lax.broadcasted_iota(jnp.int32, (slots, lane), 1)
    info = jnp.where(place == 0, per_slot(gates), 0.0)
    info = jnp.where(place == 1, coarse, info)
    info = jnp.where(place == 2, slope - coarse, info)
    info = jnp.where(place == 3, per_slot(other), info)
    info_ref[...] = info.astype(bf16)
    slots_ref[...] = dot(pick, xn, ((1,), (0,))).astype(bf16)


def cot_kernel(last_ref, arrived_ref, noise_ref, rewards_ref, pick_ref, info_ref, cot_ref, slots_ref):
    width = arrived_ref.shape[1]
    own = (-rewards_ref[...] * noise_ref[...].astype(f32)).astype(bf16)
    last = last_ref[0] == 1
    cot = jnp.where(last, own.astype(f32), arrived_ref[...].astype(f32)).astype(bf16)
    cot_ref[...] = cot
    slots_ref[:, :width] = dot(pick_ref[...], cot, ((1,), (0,))).astype(bf16)
    slots_ref[:, width:] = info_ref[...]


def in_words(value, axis):
    words = []
    for _ in range(3):
        word = value.astype(bf16).astype(f32)
        words.append(word)
        value = value - word
    return jnp.concatenate(words, axis).astype(bf16)


def from_words(value):
    rows = value.shape[0] // 3
    return value[:rows] + (value[rows : 2 * rows] + value[2 * rows :])


def expert_rows(xn, cot, info, up, down, router, mine):
    rows = xn.shape[0]
    experts = router.shape[0]
    gate = info[:, 0:1]
    pre = dot(xn, up, ((1,), (0,)))
    dh = dot(cot, down, ((1,), (1,)))
    square = pre * pre
    tangent = jnp.tanh(gelu_scale * pre * (1.0 + cubic_coef * square))
    hidden = 0.5 * pre * (1.0 + tangent)
    slope = 0.5 * (1.0 + tangent) + 0.5 * pre * (1.0 - tangent * tangent) * gelu_scale * (
        1.0 + 3.0 * cubic_coef * square
    )
    hidden = hidden.astype(bf16).astype(f32)
    d_logit = (info[:, 1:2] + info[:, 2:3]) * jnp.sum(hidden * dh, -1, keepdims=True)
    d_pre = (dh * slope * gate).astype(bf16)
    place = lax.broadcasted_iota(jnp.int32, (rows, lane), 1).astype(f32)
    sign = (place == mine.astype(f32)).astype(f32) - (place == info[:, 3:4]).astype(f32)
    d_logits = sign * d_logit
    back = dot(d_pre, up, ((1,), (1,)))
    back = back + dot(
        in_words(d_logits[:, :experts], 1), jnp.concatenate([router] * 3, 0), ((1,), (0,))
    )
    turned = d_logits.T[:experts]
    part = from_words(dot(in_words(turned, 0), xn, ((1,), (0,))))
    gain = jnp.sum(back * xn.astype(f32), 0, keepdims=True)
    return (hidden * gate).astype(bf16), d_pre, back, jnp.concatenate([part, gain], 0)


def expert_kernel(count, mine_ref, up_ref, down_ref, router_ref, before_ref, *refs):
    ins = refs[: 2 * count]
    h_ref, d_ref, part_ref = refs[2 * count : 2 * count + 3]
    outs = refs[2 * count + 3 :]
    width = up_ref.shape[0]
    cot = jnp.concatenate([ref[...] for ref in ins[count:]], 0)
    h_ref[...], d_ref[...], back, part = expert_rows(
        jnp.concatenate([ref[...] for ref in ins[:count]], 0),
        cot[:, :width],
        cot[:, width:].astype(f32),
        up_ref[...],
        down_ref[...],
        router_ref[...],
        mine_ref[0],
    )
    part_ref[...] = before_ref[...] + part
    step = outs[0].shape[0]
    for i in range(len(outs)):
        outs[i][...] = back[i * step : (i + 1) * step].astype(bf16)


def run_experts(mine, up, down, router, before, xns, cots, parts):
    total = sum(xn.shape[0] for xn in xns)
    width, hid = up.shape
    found = call(
        functools.partial(expert_kernel, len(xns)),
        [like((total, hid), bf16), like((total, hid), bf16), like(before.shape, f32)]
        + [like((total // parts, width), bf16)] * parts,
        6 * total * up.size,
        4 * up.size + 8 * total * width,
        in_specs=[scalar()] + [whole()] * (4 + 2 * len(xns)),
    )(mine, up, down, router, before, *xns, *cots)
    return found[0], found[1], found[2], found[3:]


def grads_kernel(xns, cots, hs, *refs):
    xn_refs, cot_refs = refs[:xns], refs[xns : xns + cots]
    h_refs = refs[xns + cots : xns + cots + hs]
    d_refs = refs[xns + cots + hs : xns + cots + 2 * hs]
    up_g_ref, down_g_ref = refs[-2:]

    def joined(group):
        return jnp.concatenate([ref[...] for ref in group], 0)

    up_g_ref[...] = dot(joined(xn_refs), joined(d_refs), ((0,), (0,))).astype(bf16)
    down_g_ref[...] = dot(joined(h_refs), joined(cot_refs), ((0,), (0,))).astype(bf16)


def run_grads(width, hid, xns, cots, hs, ds):
    steps = 6
    specs = [pl.BlockSpec((v.shape[0], width // steps), lambda i: (0, i)) for v in xns]
    specs += [pl.BlockSpec((v.shape[0], width), lambda i: (0, 0)) for v in cots]
    specs += [pl.BlockSpec((v.shape[0], hid // steps), lambda i: (0, i)) for v in hs]
    specs += [pl.BlockSpec((v.shape[0], hid), lambda i: (0, 0)) for v in ds]
    total = sum(v.shape[0] for v in xns)
    return call(
        functools.partial(grads_kernel, len(xns), len(cots), len(hs)),
        [like((width, hid), bf16), like((hid, width), bf16)],
        4 * total * width * hid // cheaper,
        (4 * width * hid + 6 * total * width) // cheaper,
        grid=(steps,),
        in_specs=specs,
        out_specs=[
            pl.BlockSpec((width // steps, hid), lambda i: (i, 0)),
            pl.BlockSpec((hid // steps, width), lambda i: (i, 0)),
        ],
    )(*xns, *cots, *hs, *ds)


def final_kernel(x_ref, gain_ref, cot_ref, slots_ref, back_ref, out_ref):
    x32 = x_ref[...].astype(f32)
    inv = lax.rsqrt(jnp.mean(x32 * x32, -1, keepdims=True) + norm_eps)
    xh = x32 * inv
    dxn = dot(back_ref[...], slots_ref[...], ((1,), (0,)))
    rows = dxn * gain_ref[...]
    out_ref[...] = (
        cot_ref[...].astype(f32) + inv * (rows - xh * jnp.mean(rows * xh, -1, keepdims=True))
    ).astype(bf16)


def shards(
    segment_input,
    upstream_grad,
    step_noise,
    rewards,
    routes,
    up_weight,
    down_weight,
    router_weight,
    norm_gain,
):
    tok_count = segment_input.shape[1]
    width = segment_input.shape[2]
    experts = router_weight.shape[2]
    split = lax.axis_size("x")
    top_count = routes.shape[2]
    capacity = tok_count * top_count // experts
    slots = experts * capacity
    half = slots // 2
    x = segment_input[0]
    up = up_weight[0]
    down = down_weight[0]
    router = router_weight[0].T
    pair = routes[0].T
    n_segment = lax.axis_size("segment")
    is_last = (lax.axis_index("segment") == n_segment - 1).astype(jnp.int32).reshape(1)
    mine = lax.axis_index("e").astype(jnp.int32).reshape(1)

    xn_slots, pick, info, pick_turned = call(
        functools.partial(token_kernel, capacity),
        [
            like((slots, width), bf16),
            like((slots, tok_count), bf16),
            like((slots, lane), bf16),
            like((tok_count, slots), bf16),
        ],
        2 * slots * tok_count * width,
        4 * tok_count * width + 2 * slots * width,
    )(x, norm_gain, router, pair)
    arrived = lax.ppermute(
        upstream_grad[0], "segment", [(i + 1, i) for i in range(n_segment - 1)]
    )
    def exchange(rows):
        shaped = rows.reshape(experts, capacity, rows.shape[1])
        return lax.all_to_all(shaped, "e", 0, 0, tiled=True).reshape(rows.shape)

    xn_own = exchange(xn_slots)
    cot, c_slots = call(
        cot_kernel,
        [like((tok_count, width), bf16), like((slots, width + lane), bf16)],
        2 * slots * tok_count * width,
        6 * tok_count * width + 2 * slots * width,
        in_specs=[scalar()] + [whole()] * 5,
    )(is_last, arrived, step_noise, rewards[:, None], pick, info)

    xn_own, c_slots = lax.optimization_barrier((xn_own, c_slots))
    xn_low, xn_high = shift(xn_own, "x", 1), shift(xn_own, "x", -1)
    c_own = exchange(c_slots)
    seen, from_low, from_high = forward_halves(experts + 1, xn_low, xn_high)
    c_own, seen = lax.optimization_barrier((c_own, seen))
    c_low, c_high = shift(c_own, "x", 1), shift(c_own, "x", -1)
    xn_far = [shift(from_low, "x", 1), shift(from_high, "x", -1)]
    h_own, d_own, part, (b_own,) = run_experts(
        mine, up, down, router, seen, [xn_own], [c_own], 1
    )
    c_low, c_high, b_own = lax.optimization_barrier((c_low, c_high, b_own))
    c_far = [shift(c_low[:half], "x", 1), shift(c_high[half:], "x", -1)]
    xn_low, xn_high, *xn_far = lax.optimization_barrier((xn_low, xn_high, *xn_far))
    h_near, d_near, part, (b_low, b_high) = run_experts(
        mine, up, down, router, part, [xn_low, xn_high], [c_low, c_high], 2
    )
    got_high, got_low = shift(b_low, "x", -1), shift(b_high, "x", 1)
    h_far, d_far, part, (b_far,) = run_experts(
        mine, up, down, router, part, xn_far, c_far, 1
    )
    got_far = shift(b_far, "x", 2)
    total = b_own.astype(f32) + got_far.astype(f32)
    back = (total + (got_high.astype(f32) + got_low.astype(f32))).astype(bf16)
    back_slots = exchange(back)
    up_g, down_g = run_grads(
        width,
        up.shape[1],
        [xn_own, xn_low, xn_high, *xn_far],
        [c_own, c_low, c_high, *c_far],
        [h_own, h_near, h_far],
        [d_own, d_near, d_far],
    )
    small = total_over(part)
    router_total = small[:experts]
    gain_total = small[experts] / norm_gain[0]

    input_g = call(
        final_kernel,
        like((tok_count, width), bf16),
        2 * slots * tok_count * width,
        8 * tok_count * width + 2 * slots * width,
    )(x, norm_gain, cot, back_slots, pick_turned)
    return (
        input_g[None],
        up_g[None],
        down_g[None],
        router_total.T[None],
        gain_total[None],
    )


def solution(mesh):
    experts = 8
    n_segment, n_dp = mesh.devices.shape
    grid = Mesh(
        mesh.devices.reshape(n_segment, experts, n_dp // experts), ("segment", "e", "x")
    )
    dp = ("e", "x")
    return jax.shard_map(
        shards,
        mesh=grid,
        in_specs=(
            P("segment", dp, None),
            P("segment", dp, None),
            P(dp, None),
            P(dp),
            P("segment", dp, None),
            P("segment", None, dp),
            P("segment", dp, None),
            P("segment", None, None),
            P("segment", None),
        ),
        out_specs=(
            P("segment", dp, None),
            P("segment", None, dp),
            P("segment", dp, None),
            P("segment", None, None),
            P("segment", None),
        ),
        check_vma=False,
    )
```
